32 devices in a mesh: seq: 32 (over z, y, x, core), head: 1.
Axes of the slice: x: 2, y: 2, z: 4, core: 2. Of those that a mesh axis runs over, the one named last changes fastest.
Arguments:
- tokens: bfloat16 [131072, 256], P('seq'), may hold values from -6 to 6
- fine_gain: float32 [256], replicated, may hold values from 0.1 to 1.9
- fine_gate: bfloat16 [256, 512], P(None, 'head'), may hold values from -0.375 to 0.375
- fine_value: bfloat16 [256, 512], P(None, 'head'), may hold values from -0.375 to 0.375
- fine_scans: bfloat16 [256, 512], replicated, may hold values from -0.375 to 0.375
- fine_steps: bfloat16 [256, 8], P(None, 'head'), may hold values from -0.375 to 0.375
- fine_kernel: float32 [4, 512], P(None, 'head'), may hold values from -3 to 3
- fine_taps: float32 [4, 512], replicated, may hold values from -3 to 3
- fine_bias: float32 [8], P('head'), may hold values from -3 to 1
- fine_decay: float32 [8], P('head'), may hold values from 7.6293945e-06 to 0.2
- fine_norm: float32 [512], P('head'), may hold values from 0.1 to 1.9
- fine_output: bfloat16 [512, 256], P('head'), may hold values from -0.25 to 0.25
- merge_weight: bfloat16 [1024, 1024], replicated, may hold values from -0.1875 to 0.1875
- coarse_gain: float32 [1024], replicated, may hold values from 0.1 to 1.9
- coarse_gate: bfloat16 [1024, 2048], P(None, 'head'), may hold values from -0.1875 to 0.1875
- coarse_value: bfloat16 [1024, 2048], P(None, 'head'), may hold values from -0.1875 to 0.1875
- coarse_scans: bfloat16 [1024, 512], replicated, may hold values from -0.1875 to 0.1875
- coarse_steps: bfloat16 [1024, 32], P(None, 'head'), may hold values from -0.1875 to 0.1875
- coarse_kernel: float32 [4, 2048], P(None, 'head'), may hold values from -3 to 3
- coarse_taps: float32 [4, 512], replicated, may hold values from -3 to 3
- coarse_bias: float32 [32], P('head'), may hold values from -3 to 1
- coarse_decay: float32 [32], P('head'), may hold values from 3.0517578e-05 to 0.2
- coarse_norm: float32 [2048], P('head'), may hold values from 0.1 to 1.9
- coarse_output: bfloat16 [2048, 1024], P('head'), may hold values from -0.125 to 0.125
Outputs:
- scene_tokens: bfloat16 [32768, 1024], P('seq', 'head')
The draws below stay inside these ranges and needn't reach their ends.
All inputs are finite; a program needn't handle non-finite values.
Results may differ from the reference program's by a relative error of at most 0.02.
Values may be sent and summed in bfloat16 or wider, within the bound.
A program may use at most 192 MiB of HBM per device.

```python
import math
import jax
import jax.numpy as jnp
from jax import lax

WIDTH = 256
INNER = 512
HEADS = 8
HEAD_DIM = 64
STATE = 256
COARSE_INNER = 2048
COARSE_HEADS = 32
KERNEL = 4
BLOCK = 256
ROW_PATCHES = 64
TOKENS = 131072
COARSE_WIDTH = 1024


def level_of(rng, dims, cuts, low, top_value):
    level = 1.0
    for dim, shards_of in cuts:
        steps = jax.random.uniform(jax.random.fold_in(jax.random.fold_in(rng, 6), dim), (shards_of,), jnp.float32, low / len(cuts), top_value / len(cuts))
        level = level * jnp.repeat(jnp.exp(steps), dims[dim] // shards_of).reshape((-1,) + (1,) * (len(dims) - 1 - dim))
    return level


def scatter_about(key, dims, scale, limit, split=(), kind=jnp.bfloat16):
    entries = jax.random.normal(key, dims, jnp.float32) * scale
    if len(split) > 0:
        entries = level_of(key, dims, split, -0.22, 0.18) * entries
    return jnp.clip(entries, min=-limit, max=limit).astype(kind)


def setup_inputs(seed: int = 0) -> dict:
    streams_of = jax.random.split(jax.random.key(seed), 25)
    tokens = scatter_about(streams_of[0], (TOKENS, WIDTH), 1.0, 6.0, ((0, 32),))
    fine_gain = jnp.clip(1.0 + 0.18 * jax.random.normal(streams_of[1], (WIDTH,), jnp.float32), 0.1, 1.9)
    fine_gate = scatter_about(streams_of[2], (WIDTH, INNER), WIDTH ** -0.5, 0.375)
    fine_value = scatter_about(streams_of[3], (WIDTH, INNER), WIDTH ** -0.5, 0.375)
    fine_scans = scatter_about(streams_of[4], (WIDTH, 2 * STATE), WIDTH ** -0.5, 0.375)
    fine_steps = scatter_about(streams_of[5], (WIDTH, HEADS), WIDTH ** -0.5, 0.375)
    fine_kernel = scatter_about(streams_of[6], (KERNEL, INNER), KERNEL ** -0.5, 3.0, (), jnp.float32)
    fine_taps = scatter_about(streams_of[7], (KERNEL, 2 * STATE), KERNEL ** -0.5, 3.0, (), jnp.float32)
    fine_bias = jnp.clip(jax.random.uniform(streams_of[8], (HEADS,), jnp.float32, -3.0, 1.0), -3.0, 1.0)
    fine_decay = jnp.clip(jnp.exp(jax.random.uniform(streams_of[9], (HEADS,), jnp.float32, math.log(7.62939453125e-06), math.log(0.2))), 7.62939453125e-06, 0.2)
    fine_norm = jnp.clip(1.0 + 0.18 * jax.random.normal(streams_of[10], (INNER,), jnp.float32), 0.1, 1.9)
    fine_output = scatter_about(streams_of[11], (INNER, WIDTH), INNER ** -0.5, 0.25)
    merge_weight = scatter_about(streams_of[12], (COARSE_WIDTH, COARSE_WIDTH), COARSE_WIDTH ** -0.5, 0.1875)
    coarse_gain = jnp.clip(1.0 + 0.18 * jax.random.normal(streams_of[13], (COARSE_WIDTH,), jnp.float32), 0.1, 1.9)
    coarse_gate = scatter_about(streams_of[14], (COARSE_WIDTH, COARSE_INNER), COARSE_WIDTH ** -0.5, 0.1875)
    coarse_value = scatter_about(streams_of[15], (COARSE_WIDTH, COARSE_INNER), COARSE_WIDTH ** -0.5, 0.1875)
    coarse_scans = scatter_about(streams_of[16], (COARSE_WIDTH, 2 * STATE), COARSE_WIDTH ** -0.5, 0.1875)
    coarse_steps = scatter_about(streams_of[17], (COARSE_WIDTH, COARSE_HEADS), COARSE_WIDTH ** -0.5, 0.1875)
    coarse_kernel = scatter_about(streams_of[18], (KERNEL, COARSE_INNER), KERNEL ** -0.5, 3.0, (), jnp.float32)
    coarse_taps = scatter_about(streams_of[19], (KERNEL, 2 * STATE), KERNEL ** -0.5, 3.0, (), jnp.float32)
    coarse_bias = jnp.clip(jax.random.uniform(streams_of[20], (COARSE_HEADS,), jnp.float32, -3.0, 1.0), -3.0, 1.0)
    coarse_decay = jnp.clip(jnp.exp(jax.random.uniform(streams_of[21], (COARSE_HEADS,), jnp.float32, math.log(3.0517578125e-05), math.log(0.2))), 3.0517578125e-05, 0.2)
    coarse_norm = jnp.clip(1.0 + 0.18 * jax.random.normal(streams_of[22], (COARSE_INNER,), jnp.float32), 0.1, 1.9)
    coarse_output = scatter_about(streams_of[23], (COARSE_INNER, COARSE_WIDTH), COARSE_INNER ** -0.5, 0.125)
    return dict(tokens=tokens, fine_gain=fine_gain, fine_gate=fine_gate, fine_value=fine_value, fine_scans=fine_scans, fine_steps=fine_steps, fine_kernel=fine_kernel, fine_taps=fine_taps, fine_bias=fine_bias, fine_decay=fine_decay, fine_norm=fine_norm, fine_output=fine_output, merge_weight=merge_weight, coarse_gain=coarse_gain, coarse_gate=coarse_gate, coarse_value=coarse_value, coarse_scans=coarse_scans, coarse_steps=coarse_steps, coarse_kernel=coarse_kernel, coarse_taps=coarse_taps, coarse_bias=coarse_bias, coarse_decay=coarse_decay, coarse_norm=coarse_norm, coarse_output=coarse_output)


EPSILON = 1e-05

def rms_rows(values, gain_vec):
    return values * lax.rsqrt(lax.optimization_barrier(jnp.mean(values * values, axis=-1, keepdims=True)) + EPSILON) * gain_vec

def causal_conv(inputs, kernel_rows):
    length = inputs.shape[0]
    padded = jnp.concatenate([jnp.zeros((KERNEL - 1, inputs.shape[1]), jnp.float32), inputs.astype(jnp.float32)], 0)
    summed = jnp.zeros((length, inputs.shape[1]), jnp.float32)
    for offset in range(KERNEL):
        summed = summed + padded[offset:offset + length] * kernel_rows[offset]
    return jax.nn.silu(summed)

def state_space(values, step_sizes, log_decay, input_map, output_map):
    length, heads_here, _ = values.shape
    blocks = length // BLOCK
    lower = jnp.tril(jnp.ones((BLOCK, BLOCK), dtype=bool))

    def advance(state, pieces):
        vals, dts, logs_blk, b_blk, c_blk = pieces
        cumul = jnp.cumsum(logs_blk, axis=0)
        scores = jnp.dot(c_blk, b_blk.T, preferred_element_type=jnp.float32)
        spread = cumul.T[:, :, None] - cumul.T[:, None, :]
        decays = jnp.exp(jnp.where(lower[None], spread, -jnp.inf))
        weights = (scores[None] * decays * dts.T[:, None, :]).astype(jnp.bfloat16)
        intra = jnp.einsum('hts,shp->thp', weights.astype(jnp.float32), vals.astype(jnp.float32))
        inter = jnp.einsum('tn,hpn->thp', c_blk.astype(jnp.float32), state, precision=lax.Precision.HIGHEST)
        inter = inter * jnp.exp(cumul)[:, :, None]
        tail_w = jnp.exp(cumul[-1][None, :] - cumul) * dts
        scaled = (vals.astype(jnp.float32) * tail_w[:, :, None]).astype(jnp.bfloat16)
        local = jnp.einsum('shp,sn->hpn', scaled.astype(jnp.float32), b_blk.astype(jnp.float32))
        state = jnp.exp(cumul[-1])[:, None, None] * state + local
        return (state, intra + inter)
    pieces = (values.reshape(blocks, BLOCK, heads_here, HEAD_DIM), step_sizes.reshape(blocks, BLOCK, heads_here), log_decay.reshape(blocks, BLOCK, heads_here), input_map.reshape(blocks, BLOCK, STATE), output_map.reshape(blocks, BLOCK, STATE))
    _, result = lax.scan(advance, jnp.zeros((heads_here, HEAD_DIM, STATE), jnp.float32), pieces)
    return result.reshape(length, heads_here * HEAD_DIM)

def mamba_branch(stream, gain_vec, gate_weight, value_weight, scan_weight, step_weight, kernel_value, kernel_scan, step_bias, decay_rate, norm_gain, out_weight):
    normed = rms_rows(stream.astype(jnp.float32), gain_vec).astype(jnp.bfloat16)
    gate_rows = jnp.dot(normed, gate_weight, preferred_element_type=jnp.float32).astype(jnp.bfloat16)
    value_rows = jnp.dot(normed, value_weight, preferred_element_type=jnp.float32).astype(jnp.bfloat16)
    scan_rows = jnp.dot(normed, scan_weight, preferred_element_type=jnp.float32).astype(jnp.bfloat16)
    step_raw = jnp.dot(normed, step_weight, preferred_element_type=jnp.float32)
    conv_values = causal_conv(value_rows, kernel_value).astype(jnp.bfloat16)
    conv_scans = causal_conv(scan_rows, kernel_scan).astype(jnp.bfloat16)
    step_sizes = jax.nn.softplus(step_raw + step_bias)
    log_decay = -step_sizes * decay_rate
    heads_here = step_sizes.shape[1]
    mixed_rows = state_space(conv_values.reshape(-1, heads_here, HEAD_DIM), step_sizes, log_decay, conv_scans[:, :STATE], conv_scans[:, STATE:])
    gated_rows = mixed_rows * jax.nn.silu(gate_rows.astype(jnp.float32))
    normed_out = rms_rows(gated_rows, norm_gain).astype(jnp.bfloat16)
    return jnp.dot(normed_out, out_weight, preferred_element_type=jnp.float32)

def merge_tiles(rows):
    count, width_here = rows.shape
    grid = rows.reshape(count // (2 * ROW_PATCHES), 2, ROW_PATCHES // 2, 2, width_here)
    return grid.transpose(0, 2, 1, 3, 4).reshape(count // 4, 4 * width_here)

def reference(tokens, fine_gain, fine_gate, fine_value, fine_scans, fine_steps, fine_kernel, fine_taps, fine_bias, fine_decay, fine_norm, fine_output, merge_weight, coarse_gain, coarse_gate, coarse_value, coarse_scans, coarse_steps, coarse_kernel, coarse_taps, coarse_bias, coarse_decay, coarse_norm, coarse_output):
    branch = mamba_branch(tokens, fine_gain, fine_gate, fine_value, fine_scans, fine_steps, fine_kernel, fine_taps, fine_bias, fine_decay, fine_norm, fine_output)
    hidden = (tokens.astype(jnp.float32) + branch).astype(jnp.bfloat16)
    tiles = merge_tiles(hidden)
    merged = jnp.dot(tiles, merge_weight, preferred_element_type=jnp.float32).astype(jnp.bfloat16)
    branch_two = mamba_branch(merged, coarse_gain, coarse_gate, coarse_value, coarse_scans, coarse_steps, coarse_kernel, coarse_taps, coarse_bias, coarse_decay, coarse_norm, coarse_output)
    return (merged.astype(jnp.float32) + branch_two).astype(jnp.bfloat16)
```

```python
import functools

import jax
import jax.numpy as jnp
from jax import lax
from jax.experimental import pallas as pl
from jax.experimental.pallas import tpu as pltpu
from jax.sharding import PartitionSpec as P

HEAD_DIM = 64
BLOCK = 256
ROW_PATCHES = 64
LANES = 128
RIM = 16
EPSILON = 1e-05
VMEM_LIMIT = 48 * 1024 * 1024
F32 = jnp.float32
BF16 = jnp.bfloat16


def whole(shape):
    return pl.BlockSpec(shape, lambda i: (0,) * len(shape), pipeline_mode=pl.Buffered(1))


def rows_of(width):
    return pl.BlockSpec((BLOCK, width), lambda i: (i, 0))


def params():
    return pltpu.CompilerParams(
        dimension_semantics=("arbitrary",), vmem_limit_bytes=VMEM_LIMIT
    )


def rms(values, gain):
    mean = jnp.mean(values * values, axis=-1, keepdims=True)
    return values * lax.rsqrt(mean + EPSILON) * gain


def silu(v):
    half = 0.5 * v
    return half + half * jnp.tanh(half)


def head_groups(heads):
    per = LANES // HEAD_DIM
    if heads % per:
        per = 1
    return per, heads // per


def over_lanes(columns, first, per):
    n = columns.shape[0]
    width = per * HEAD_DIM
    lane = lax.broadcasted_iota(jnp.int32, (n, width), 1)
    out = jnp.broadcast_to(columns[:, first : first + 1], (n, width))
    for k in range(1, per):
        out = jnp.where(lane >= k * HEAD_DIM, columns[:, first + k : first + k + 1], out)
    return out


def to_columns(by_head):
    heads = by_head.shape[0]
    if heads < LANES:
        by_head = jnp.concatenate([by_head, jnp.zeros((LANES - heads, BLOCK), F32)], 0)
    return by_head.T


def dot(a, b):
    return jnp.dot(a, b, preferred_element_type=F32)


def dot_t(a, b):
    return lax.dot_general(a, b, (((1,), (1,)), ((), ())), preferred_element_type=F32)


def first_kernel(merging, heads, taps_count, slab, *refs):
    if merging:
        x_ref, rim_ref, merge_ref, *refs = refs
    else:
        x_ref, rim_ref, *refs = refs
        merge_ref = None
    (gain_ref, value_ref, scans_ref, steps_ref, kernel_ref, taps_ref, bias_ref, decay_ref, *refs) = refs
    if merging:
        merged_ref, *refs = refs
    (xv_ref, bc_ref, pack_ref, prefix_ref, ext_ref, raw, state, scaled, before, total) = refs
    step = pl.program_id(0)
    inner = value_ref.shape[1]
    both = scans_ref.shape[1]
    state_n = both // 2
    padded = steps_ref.shape[0]

    def project(rows):
        if merging:
            rows = dot(rows, merge_ref[...]).astype(BF16)
        normed = rms(rows.astype(F32), gain_ref[...]).astype(BF16)
        return rows, normed

    def rounded(normed, weight):
        return dot(normed, weight).astype(BF16).astype(F32)

    @pl.when(step == 0)
    def _():
        _, normed = project(rim_ref[...])
        raw[0:8, :inner] = rounded(normed, value_ref[...])[RIM - 8 :]
        raw[0:8, inner:] = rounded(normed, scans_ref[...])[RIM - 8 :]
        state[...] = jnp.zeros_like(state)
        before[...] = jnp.zeros_like(before)
        total[...] = jnp.zeros_like(total)

    @pl.when(step > 0)
    def _():
        raw[0:8, :] = raw[BLOCK : BLOCK + 8, :]

    rows, normed = project(x_ref[...])
    if merging:
        merged_ref[...] = rows
    raw[8 : 8 + BLOCK, :inner] = rounded(normed, value_ref[...])
    raw[8 : 8 + BLOCK, inner:] = rounded(normed, scans_ref[...])

    def convolved(start, width, taps):
        summed = None
        for k in range(taps_count):
            at = 8 - (taps_count - 1) + k
            term = raw[at : at + BLOCK, start : start + width] * taps[k : k + 1, :]
            summed = term if summed is None else summed + term
        return silu(summed).astype(BF16)

    for start in range(0, both, LANES):
        bc_ref[:, start : start + LANES] = convolved(
            inner + start, LANES, taps_ref[:, start : start + LANES]
        )

    raw_steps = dot_t(steps_ref[...], normed) + bias_ref[:, 0:1]
    sizes = jnp.maximum(raw_steps, 0.0) + jnp.log1p(jnp.exp(-jnp.abs(raw_steps)))
    logs = -sizes * decay_ref[:, 0:1]
    upper = (
        lax.broadcasted_iota(jnp.int32, (BLOCK, BLOCK), 0)
        <= lax.broadcasted_iota(jnp.int32, (BLOCK, BLOCK), 1)
    ).astype(F32)
    cumul = jnp.dot(logs, upper, preferred_element_type=F32, precision=lax.Precision.HIGHEST)
    last = cumul[:, BLOCK - 1 : BLOCK]
    tail = jnp.exp(last - cumul) * sizes
    pack_ref[0, 0:padded, :] = cumul
    pack_ref[0, padded : 2 * padded, :] = jnp.log(sizes) - cumul
    pack_ref[0, 2 * padded : 3 * padded, :] = cumul + before[:, 0:1]
    before[...] = before[...] + last
    tail_columns = to_columns(tail)
    last_row = to_columns(cumul)[BLOCK - 1 : BLOCK, :]
    total[...] = total[...] + last_row
    kept = jnp.exp(last_row)

    per, groups = head_groups(heads)
    width = per * HEAD_DIM
    for g in range(groups):
        lanes = slice(g * width, (g + 1) * width)
        values = convolved(g * width, width, kernel_ref[:, lanes])
        xv_ref[:, lanes] = values
        scaled[:, lanes] = (
            values.astype(F32) * over_lanes(tail_columns, g * per, per)
        ).astype(BF16)
    prefix_ref[0] = state[...].astype(BF16)
    local = lax.dot_general(
        bc_ref[:, :state_n], scaled[...], (((0,), (0,)), ((), ())), preferred_element_type=F32
    )
    for g in range(groups):
        lanes = slice(g * width, (g + 1) * width)
        state[:, lanes] = state[:, lanes] * over_lanes(kept, g * per, per) + local[:, lanes]

    @pl.when(step == pl.num_programs(0) - 1)
    def _():
        ext_ref[:, :inner] = state[...].astype(BF16)
        part = lax.broadcasted_iota(jnp.int32, (state_n, LANES), 0) % slab
        sums = jnp.broadcast_to(total[...], (state_n, LANES))
        high = sums.astype(BF16).astype(F32)
        middle = (sums - high).astype(BF16).astype(F32)
        low = sums - high - middle
        ext_ref[:, inner:] = jnp.where(
            part == 0, high, jnp.where(part == 1, middle, jnp.where(part == 2, low, 0.0))
        ).astype(BF16)


def second_kernel(heads, stream_ref, gain_ref, gate_ref, xv_ref, bc_ref, pack_ref, prefix_ref, sg_ref, mixed_ref):
    state_n = bc_ref.shape[1] // 2
    padded = pack_ref.shape[1] // 3
    normed = rms(stream_ref[...].astype(F32), gain_ref[...]).astype(BF16)
    gate_rows = dot(normed, gate_ref[...]).astype(BF16).astype(F32)
    sg_ref[...] = silu(gate_rows).astype(BF16)
    b_map, c_map = bc_ref[:, :state_n], bc_ref[:, state_n:]
    lower = lax.broadcasted_iota(jnp.int32, (BLOCK, BLOCK), 0) >= lax.broadcasted_iota(
        jnp.int32, (BLOCK, BLOCK), 1
    )
    scores = jnp.where(lower, dot_t(c_map, b_map), 0.0)
    columns = to_columns(pack_ref[0, 0:padded, :])
    grown = jnp.exp(columns)
    earlier = dot(c_map, prefix_ref[0])
    per, groups = head_groups(heads)
    width = per * HEAD_DIM
    lane = lax.broadcasted_iota(jnp.int32, (BLOCK, width), 1)
    for g in range(groups):
        lanes = slice(g * width, (g + 1) * width)
        values = xv_ref[:, lanes]
        intra = None
        for k in range(per):
            h = g * per + k
            spread = columns[:, h : h + 1] + pack_ref[0, padded + h : padded + h + 1, :]
            weights = (jnp.exp(jnp.where(lower, spread, -1e30)) * scores).astype(BF16)
            piece = dot(weights, values)
            intra = piece if k == 0 else jnp.where(lane >= k * HEAD_DIM, piece, intra)
        mixed_ref[:, lanes] = (
            intra + earlier[:, lanes] * over_lanes(grown, g * per, per)
        ).astype(BF16)


def third_kernel(heads, finish, tiling, inner_total, stream_ref, sg_ref, mixed_ref, c_ref, pack_ref, incoming_ref, norm_ref, output_ref, *refs):
    padded = pack_ref.shape[1] // 3
    if finish:
        out_ref, gated_s, *hidden_s = refs
    else:
        out_ref, squares_ref, gated_s = refs
    grown = jnp.exp(to_columns(pack_ref[0, 2 * padded : 3 * padded, :]))
    carried = dot(c_ref[...], incoming_ref[...])
    per, groups = head_groups(heads)
    width = per * HEAD_DIM
    squares = None
    for g in range(groups):
        lanes = slice(g * width, (g + 1) * width)
        mixed = mixed_ref[:, lanes].astype(F32) + carried[:, lanes] * over_lanes(grown, g * per, per)
        gated = mixed * sg_ref[:, lanes].astype(F32)
        squares = gated * gated if squares is None else squares + gated * gated
        gated_s[:, lanes] = (gated * norm_ref[:, lanes]).astype(BF16)
    squares = jnp.sum(squares, axis=1, keepdims=True)
    branch = dot(gated_s[...], output_ref[...])
    if not finish:
        out_ref[...] = branch
        squares_ref[...] = jnp.broadcast_to(squares, (BLOCK, LANES))
        return
    branch = branch * lax.rsqrt(squares / inner_total + EPSILON)
    result = stream_ref[...].astype(F32) + branch
    if not tiling:
        out_ref[...] = result.astype(BF16)
        return
    hidden = hidden_s[0]
    features = result.shape[1]
    half = ROW_PATCHES // 2
    for c in range(features // LANES):
        hidden[c] = result[:, c * LANES : (c + 1) * LANES]
    for pair in range(BLOCK // (2 * ROW_PATCHES)):
        for i in range(2):
            for j in range(2):
                start = (2 * pair + i) * ROW_PATCHES + j
                for c in range(features // LANES):
                    at = (2 * i + j) * features + c * LANES
                    out_ref[pair * half : (pair + 1) * half, at : at + LANES] = hidden[
                        c, pl.ds(start, half, stride=2), :
                    ].astype(BF16)


def prefix_kernel(ext_ref, out_ref):
    count, slab, inner = out_ref.shape
    sums = jnp.sum(ext_ref[:, :, inner:].astype(F32), axis=1)
    spread = (
        lax.broadcasted_iota(jnp.int32, (LANES, inner), 0)
        == lax.broadcasted_iota(jnp.int32, (LANES, inner), 1) // HEAD_DIM
    ).astype(F32)
    kept = jnp.dot(
        jnp.exp(sums), spread, preferred_element_type=F32, precision=lax.Precision.HIGHEST
    )
    carried = jnp.zeros((slab, inner), F32)
    for k in range(count):
        out_ref[k] = carried.astype(BF16)
        carried = carried * kept[k : k + 1, :] + ext_ref[k, :, :inner].astype(F32)


def passed_along(block, axis, distance):
    devices = range(lax.axis_size(axis))
    route = [(i - distance, i) for i in devices if i - distance in devices]
    return lax.ppermute(block, axis, route)


def mamba(
    rows,
    merge_weight,
    gain_vec,
    gate_weight,
    value_weight,
    scan_weight,
    step_weight,
    kernel_value,
    kernel_scan,
    step_bias,
    decay_rate,
    norm_gain,
    out_weight,
    tiling,
):
    length, wide = rows.shape
    inner = value_weight.shape[1]
    heads = step_weight.shape[1]
    both = scan_weight.shape[1]
    state_n = both // 2
    taps_count = kernel_value.shape[0]
    features = out_weight.shape[1]
    blocks = length // BLOCK
    seq, shares = lax.axis_size("seq"), lax.axis_size("head")
    slab = state_n // seq
    padded = -(-heads // 8) * 8
    merging = merge_weight is not None
    extra = padded - heads
    steps_t = jnp.pad(step_weight.T, ((0, extra), (0, 0)))
    bias = jnp.broadcast_to(jnp.pad(step_bias, (0, extra))[:, None], (padded, LANES))
    decay = jnp.broadcast_to(jnp.pad(decay_rate, (0, extra))[:, None], (padded, LANES))
    gain = gain_vec[None, :]
    rim = passed_along(rows[length - RIM :], "seq", 1)

    shape = jax.ShapeDtypeStruct
    ins = [rows, rim] + ([merge_weight] if merging else [])
    ins += [gain, value_weight, scan_weight, steps_t, kernel_value, kernel_scan, bias, decay]
    outs = [shape((length, features), BF16)] if merging else []
    out_specs = [rows_of(features)] if merging else []
    outs += [
        shape((length, inner), BF16),
        shape((length, both), BF16),
        shape((blocks, 3 * padded, BLOCK), F32),
        shape((blocks, state_n, inner), BF16),
        shape((state_n, inner + LANES), BF16),
    ]
    pack_spec = pl.BlockSpec((1, 3 * padded, BLOCK), lambda i: (i, 0, 0))
    prefix_spec = pl.BlockSpec((1, state_n, inner), lambda i: (i, 0, 0))
    out_specs += [
        rows_of(inner),
        rows_of(both),
        pack_spec,
        prefix_spec,
        whole((state_n, inner + LANES)),
    ]
    made = pl.pallas_call(
        functools.partial(first_kernel, merging, heads, taps_count, slab),
        grid=(blocks,),
        in_specs=[rows_of(wide)] + [whole(a.shape) for a in ins[1:]],
        out_specs=out_specs,
        out_shape=outs,
        scratch_shapes=[
            pltpu.VMEM((BLOCK + 8, inner + both), F32),
            pltpu.VMEM((state_n, inner), F32),
            pltpu.VMEM((BLOCK, inner), BF16),
            pltpu.VMEM((padded, LANES), F32),
            pltpu.VMEM((1, LANES), F32),
        ],
        compiler_params=params(),
        name="first_merge" if merging else "first",
    )(*ins)
    stream = made[0] if merging else rows
    xv, bc, pack, prefix, ext = made[-5:]

    spread_out = lax.all_to_all(
        ext.reshape(seq, slab, inner + LANES), "seq", 0, 0, tiled=True
    )

    flops = 2 * length * (features * inner + inner * (BLOCK * 4 + state_n) + BLOCK * state_n)
    sg, mixed = pl.pallas_call(
        functools.partial(second_kernel, heads),
        grid=(blocks,),
        in_specs=[
            rows_of(features),
            whole(gain.shape),
            whole(gate_weight.shape),
            rows_of(inner),
            rows_of(both),
            pack_spec,
            prefix_spec,
        ],
        out_specs=[rows_of(inner), rows_of(inner)],
        out_shape=[shape((length, inner), BF16), shape((length, inner), BF16)],
        compiler_params=params(),
        cost_estimate=pl.CostEstimate(
            flops=flops, bytes_accessed=12 * length * inner, transcendentals=length * heads * BLOCK
        ),
        name="second",
    )(stream, gain, gate_weight, xv, bc, pack, prefix)

    before = pl.pallas_call(
        prefix_kernel,
        out_shape=shape((seq, slab, inner), BF16),
        in_specs=[pl.BlockSpec(memory_space=pltpu.VMEM)],
        out_specs=pl.BlockSpec(memory_space=pltpu.VMEM),
        compiler_params=pltpu.CompilerParams(vmem_limit_bytes=VMEM_LIMIT),
        name="prefix",
    )(spread_out)
    incoming = lax.all_to_all(before, "seq", 0, 0, tiled=True).reshape(state_n, inner)

    norm = norm_gain[None, :]
    finish = shares == 1
    scratch = [pltpu.VMEM((BLOCK, inner), BF16)]
    if not finish:
        outs = [shape((length, features), F32), shape((length, LANES), F32)]
        out_specs = [rows_of(features), rows_of(LANES)]
    elif tiling:
        outs = shape((length // 4, 4 * features), BF16)
        out_specs = pl.BlockSpec((BLOCK // 4, 4 * features), lambda i: (i, 0))
        scratch += [pltpu.VMEM((features // LANES, BLOCK, LANES), F32)]
    else:
        outs, out_specs = shape((length, features), BF16), rows_of(features)
    result = pl.pallas_call(
        functools.partial(third_kernel, heads, finish, tiling, inner * shares),
        grid=(blocks,),
        in_specs=[
            rows_of(features),
            rows_of(inner),
            rows_of(inner),
            pl.BlockSpec((BLOCK, state_n), lambda i: (i, 1)),
            pack_spec,
            whole((state_n, inner)),
            whole(norm.shape),
            whole(out_weight.shape),
        ],
        out_specs=out_specs,
        out_shape=outs,
        scratch_shapes=scratch,
        compiler_params=params(),
        name="third_tiles" if tiling else "third",
    )(stream, sg, mixed, bc, pack, incoming, norm, out_weight)
    if finish:
        return result
    branch, squares = result
    mean = lax.psum(squares[:, :1], "head") / (inner * shares)
    branch = (branch * lax.rsqrt(mean + EPSILON)).astype(BF16)
    if tiling:
        summed = lax.psum(branch, "head").astype(F32)
        return merge_tiles((stream.astype(F32) + summed).astype(BF16))
    summed = lax.psum_scatter(branch, "head", scatter_dimension=1, tiled=True).astype(F32)
    share = features // shares
    mine = lax.dynamic_slice_in_dim(stream, lax.axis_index("head") * share, share, 1)
    return (mine.astype(F32) + summed).astype(BF16)


def merge_tiles(rows):
    count, width_here = rows.shape
    grid = rows.reshape(count // (2 * ROW_PATCHES), 2, ROW_PATCHES // 2, 2, width_here)
    return grid.transpose(0, 2, 1, 3, 4).reshape(count // 4, 4 * width_here)


def shards(tokens, *weights):
    tiles = mamba(tokens, None, *weights[:11], True)
    return mamba(tiles, weights[11], *weights[12:], False)


def solution(mesh):
    return jax.shard_map(
        shards,
        mesh=mesh,
        in_specs=(
            P("seq", None),
            P(),
            P(None, "head"),
            P(None, "head"),
            P(),
            P(None, "head"),
            P(None, "head"),
            P(),
            P("head"),
            P("head"),
            P("head"),
            P("head", None),
            P(),
            P(),
            P(None, "head"),
            P(None, "head"),
            P(),
            P(None, "head"),
            P(None, "head"),
            P(),
            P("head"),
            P("head"),
            P("head"),
            P("head", None),
        ),
        out_specs=P("seq", "head"),
        check_vma=False,
    )
```

```python
import functools

import jax
import jax.numpy as jnp
from jax import lax
from jax.experimental import pallas as pl
from jax.experimental.pallas import tpu as pltpu
from jax.sharding import PartitionSpec as P

HEAD_DIM = 64
BLOCK = 256
ROW_PATCHES = 64
LANES = 128
RIM = 16
EPSILON = 1e-05
VMEM_LIMIT = 48 * 1024 * 1024
F32 = jnp.float32
BF16 = jnp.bfloat16


def whole(shape):
    return pl.BlockSpec(shape, lambda i: (0,) * len(shape), pipeline_mode=pl.Buffered(1))


def rows_of(width):
    return pl.BlockSpec((BLOCK, width), lambda i: (i, 0))


def params():
    return pltpu.CompilerParams(
        dimension_semantics=("arbitrary",), vmem_limit_bytes=VMEM_LIMIT
    )


def rms(values, gain):
    mean = jnp.mean(values * values, axis=-1, keepdims=True)
    return values * lax.rsqrt(mean + EPSILON) * gain


def silu(v):
    half = 0.5 * v
    return half + half * jnp.tanh(half)


def head_groups(heads):
    per = LANES // HEAD_DIM
    if heads % per:
        per = 1
    return per, heads // per


def over_lanes(columns, first, per):
    n = columns.shape[0]
    width = per * HEAD_DIM
    lane = lax.broadcasted_iota(jnp.int32, (n, width), 1)
    out = jnp.broadcast_to(columns[:, first : first + 1], (n, width))
    for k in range(1, per):
        out = jnp.where(lane >= k * HEAD_DIM, columns[:, first + k : first + k + 1], out)
    return out


def to_columns(by_head):
    heads = by_head.shape[0]
    if heads < LANES:
        by_head = jnp.concatenate([by_head, jnp.zeros((LANES - heads, BLOCK), F32)], 0)
    return by_head.T


def dot(a, b):
    return jnp.dot(a, b, preferred_element_type=F32)


def dot_t(a, b):
    return lax.dot_general(a, b, (((1,), (1,)), ((), ())), preferred_element_type=F32)


def first_kernel(merging, heads, taps_count, slab, *refs):
    if merging:
        x_ref, rim_ref, merge_ref, *refs = refs
    else:
        x_ref, rim_ref, *refs = refs
        merge_ref = None
    (gain_ref, value_ref, scans_ref, steps_ref, kernel_ref, taps_ref, bias_ref, decay_ref, *refs) = refs
    if merging:
        merged_ref, *refs = refs
    (xv_ref, bc_ref, pack_ref, prefix_ref, ext_ref, raw, state, scaled, before, total) = refs
    step = pl.program_id(0)
    inner = value_ref.shape[1]
    both = scans_ref.shape[1]
    state_n = both // 2
    padded = steps_ref.shape[0]

    def project(rows):
        if merging:
            rows = dot(rows, merge_ref[...]).astype(BF16)
        normed = rms(rows.astype(F32), gain_ref[...]).astype(BF16)
        return rows, normed

    def rounded(normed, weight):
        return dot(normed, weight).astype(BF16).astype(F32)

    @pl.when(step == 0)
    def _():
        _, normed = project(rim_ref[...])
        raw[0:8, :inner] = rounded(normed, value_ref[...])[RIM - 8 :]
        raw[0:8, inner:] = rounded(normed, scans_ref[...])[RIM - 8 :]
        state[...] = jnp.zeros_like(state)
        before[...] = jnp.zeros_like(before)
        total[...] = jnp.zeros_like(total)

    @pl.when(step > 0)
    def _():
        raw[0:8, :] = raw[BLOCK : BLOCK + 8, :]

    rows, normed = project(x_ref[...])
    if merging:
        merged_ref[...] = rows
    raw[8 : 8 + BLOCK, :inner] = rounded(normed, value_ref[...])
    raw[8 : 8 + BLOCK, inner:] = rounded(normed, scans_ref[...])

    def convolved(start, width, taps):
        summed = None
        for k in range(taps_count):
            at = 8 - (taps_count - 1) + k
            term = raw[at : at + BLOCK, start : start + width] * taps[k : k + 1, :]
            summed = term if summed is None else summed + term
        return silu(summed).astype(BF16)

    for start in range(0, both, LANES):
        bc_ref[:, start : start + LANES] = convolved(
            inner + start, LANES, taps_ref[:, start : start + LANES]
        )

    raw_steps = dot_t(steps_ref[...], normed) + bias_ref[:, 0:1]
    sizes = jnp.maximum(raw_steps, 0.0) + jnp.log1p(jnp.exp(-jnp.abs(raw_steps)))
    logs = -sizes * decay_ref[:, 0:1]
    upper = (
        lax.broadcasted_iota(jnp.int32, (BLOCK, BLOCK), 0)
        <= lax.broadcasted_iota(jnp.int32, (BLOCK, BLOCK), 1)
    ).astype(F32)
    cumul = jnp.dot(logs, upper, preferred_element_type=F32, precision=lax.Precision.HIGHEST)
    last = cumul[:, BLOCK - 1 : BLOCK]
    tail = jnp.exp(last - cumul) * sizes
    pack_ref[0, 0:padded, :] = cumul
    pack_ref[0, padded : 2 * padded, :] = jnp.log(sizes) - cumul
    pack_ref[0, 2 * padded : 3 * padded, :] = cumul + before[:, 0:1]
    before[...] = before[...] + last
    tail_columns = to_columns(tail)
    last_row = to_columns(cumul)[BLOCK - 1 : BLOCK, :]
    total[...] = total[...] + last_row
    kept = jnp.exp(last_row)

    per, groups = head_groups(heads)
    width = per * HEAD_DIM
    for g in range(groups):
        lanes = slice(g * width, (g + 1) * width)
        values = convolved(g * width, width, kernel_ref[:, lanes])
        xv_ref[:, lanes] = values
        scaled[:, lanes] = (
            values.astype(F32) * over_lanes(tail_columns, g * per, per)
        ).astype(BF16)
    prefix_ref[0] = state[...].astype(BF16)
    local = lax.dot_general(
        bc_ref[:, :state_n], scaled[...], (((0,), (0,)), ((), ())), preferred_element_type=F32
    )
    for g in range(groups):
        lanes = slice(g * width, (g + 1) * width)
        state[:, lanes] = state[:, lanes] * over_lanes(kept, g * per, per) + local[:, lanes]

    @pl.when(step == pl.num_programs(0) - 1)
    def _():
        ext_ref[:, :inner] = state[...].astype(BF16)
        part = lax.broadcasted_iota(jnp.int32, (state_n, LANES), 0) % slab
        sums = jnp.broadcast_to(total[...], (state_n, LANES))
        high = sums.astype(BF16).astype(F32)
        middle = (sums - high).astype(BF16).astype(F32)
        low = sums - high - middle
        ext_ref[:, inner:] = jnp.where(
            part == 0, high, jnp.where(part == 1, middle, jnp.where(part == 2, low, 0.0))
        ).astype(BF16)


def second_kernel(heads, kept, *refs):
    stream_ref, gain_ref, gate_ref, xv_ref, bc_ref, pack_ref, prefix_ref, sg_ref, mixed_ref = refs[kept:]
    state_n = bc_ref.shape[1] // 2
    padded = pack_ref.shape[1] // 3
    normed = rms(stream_ref[...].astype(F32), gain_ref[...]).astype(BF16)
    gate_rows = dot(normed, gate_ref[...]).astype(BF16).astype(F32)
    sg_ref[...] = silu(gate_rows).astype(BF16)
    b_map, c_map = bc_ref[:, :state_n], bc_ref[:, state_n:]
    lower = lax.broadcasted_iota(jnp.int32, (BLOCK, BLOCK), 0) >= lax.broadcasted_iota(
        jnp.int32, (BLOCK, BLOCK), 1
    )
    scores = jnp.where(lower, dot_t(c_map, b_map), 0.0)
    columns = to_columns(pack_ref[0, 0:padded, :])
    grown = jnp.exp(columns)
    earlier = dot(c_map, prefix_ref[0])
    per, groups = head_groups(heads)
    width = per * HEAD_DIM
    lane = lax.broadcasted_iota(jnp.int32, (BLOCK, width), 1)
    for g in range(groups):
        lanes = slice(g * width, (g + 1) * width)
        values = xv_ref[:, lanes]
        intra = None
        for k in range(per):
            h = g * per + k
            spread = columns[:, h : h + 1] + pack_ref[0, padded + h : padded + h + 1, :]
            weights = (jnp.exp(jnp.where(lower, spread, -1e30)) * scores).astype(BF16)
            piece = dot(weights, values)
            intra = piece if k == 0 else jnp.where(lane >= k * HEAD_DIM, piece, intra)
        mixed_ref[:, lanes] = (
            intra + earlier[:, lanes] * over_lanes(grown, g * per, per)
        ).astype(BF16)


def third_kernel(heads, finish, tiling, inner_total, stream_ref, sg_ref, mixed_ref, c_ref, pack_ref, incoming_ref, norm_ref, output_ref, *refs):
    padded = pack_ref.shape[1] // 3
    if finish:
        out_ref, gated_s, *hidden_s = refs
    else:
        out_ref, squares_ref, gated_s = refs
    grown = jnp.exp(to_columns(pack_ref[0, 2 * padded : 3 * padded, :]))
    carried = dot(c_ref[...], incoming_ref[...])
    per, groups = head_groups(heads)
    width = per * HEAD_DIM
    squares = None
    for g in range(groups):
        lanes = slice(g * width, (g + 1) * width)
        mixed = mixed_ref[:, lanes].astype(F32) + carried[:, lanes] * over_lanes(grown, g * per, per)
        gated = mixed * sg_ref[:, lanes].astype(F32)
        squares = gated * gated if squares is None else squares + gated * gated
        gated_s[:, lanes] = (gated * norm_ref[:, lanes]).astype(BF16)
    squares = jnp.sum(squares, axis=1, keepdims=True)
    branch = dot(gated_s[...], output_ref[...])
    if not finish:
        out_ref[...] = branch
        squares_ref[...] = jnp.broadcast_to(squares, (BLOCK, LANES))
        return
    branch = branch * lax.rsqrt(squares / inner_total + EPSILON)
    result = stream_ref[...].astype(F32) + branch
    if not tiling:
        out_ref[...] = result.astype(BF16)
        return
    hidden = hidden_s[0]
    features = result.shape[1]
    half = ROW_PATCHES // 2
    for c in range(features // LANES):
        hidden[c] = result[:, c * LANES : (c + 1) * LANES]
    for pair in range(BLOCK // (2 * ROW_PATCHES)):
        for i in range(2):
            for j in range(2):
                start = (2 * pair + i) * ROW_PATCHES + j
                for c in range(features // LANES):
                    at = (2 * i + j) * features + c * LANES
                    out_ref[pair * half : (pair + 1) * half, at : at + LANES] = hidden[
                        c, pl.ds(start, half, stride=2), :
                    ].astype(BF16)


def prefix_kernel(ext_ref, out_ref):
    count, slab, inner = out_ref.shape
    sums = jnp.sum(ext_ref[:, :, inner:].astype(F32), axis=1)
    spread = (
        lax.broadcasted_iota(jnp.int32, (LANES, inner), 0)
        == lax.broadcasted_iota(jnp.int32, (LANES, inner), 1) // HEAD_DIM
    ).astype(F32)
    kept = jnp.dot(
        jnp.exp(sums), spread, preferred_element_type=F32, precision=lax.Precision.HIGHEST
    )
    carried = jnp.zeros((slab, inner), F32)
    for k in range(count):
        out_ref[k] = carried.astype(BF16)
        carried = carried * kept[k : k + 1, :] + ext_ref[k, :, :inner].astype(F32)


def passed_along(block, axis, distance):
    devices = range(lax.axis_size(axis))
    route = [(i - distance, i) for i in devices if i - distance in devices]
    return lax.ppermute(block, axis, route)


def mamba(
    rows,
    merge_weight,
    gain_vec,
    gate_weight,
    value_weight,
    scan_weight,
    step_weight,
    kernel_value,
    kernel_scan,
    step_bias,
    decay_rate,
    norm_gain,
    out_weight,
    tiling,
):
    length, wide = rows.shape
    inner = value_weight.shape[1]
    heads = step_weight.shape[1]
    both = scan_weight.shape[1]
    state_n = both // 2
    taps_count = kernel_value.shape[0]
    features = out_weight.shape[1]
    blocks = length // BLOCK
    seq, shares = lax.axis_size("seq"), lax.axis_size("head")
    slab = state_n // seq
    padded = -(-heads // 8) * 8
    merging = merge_weight is not None
    extra = padded - heads
    steps_t = jnp.pad(step_weight.T, ((0, extra), (0, 0)))
    bias = jnp.broadcast_to(jnp.pad(step_bias, (0, extra))[:, None], (padded, LANES))
    decay = jnp.broadcast_to(jnp.pad(decay_rate, (0, extra))[:, None], (padded, LANES))
    gain = gain_vec[None, :]
    rim = passed_along(rows[length - RIM :], "seq", 1)

    shape = jax.ShapeDtypeStruct
    ins = [rows, rim] + ([merge_weight] if merging else [])
    ins += [gain, value_weight, scan_weight, steps_t, kernel_value, kernel_scan, bias, decay]
    outs = [shape((length, features), BF16)] if merging else []
    out_specs = [rows_of(features)] if merging else []
    outs += [
        shape((length, inner), BF16),
        shape((length, both), BF16),
        shape((blocks, 3 * padded, BLOCK), F32),
        shape((blocks, state_n, inner), BF16),
        shape((state_n, inner + LANES), BF16),
    ]
    pack_spec = pl.BlockSpec((1, 3 * padded, BLOCK), lambda i: (i, 0, 0))
    prefix_spec = pl.BlockSpec((1, state_n, inner), lambda i: (i, 0, 0))
    out_specs += [
        rows_of(inner),
        rows_of(both),
        pack_spec,
        prefix_spec,
        whole((state_n, inner + LANES)),
    ]
    made = pl.pallas_call(
        functools.partial(first_kernel, merging, heads, taps_count, slab),
        grid=(blocks,),
        in_specs=[rows_of(wide)] + [whole(a.shape) for a in ins[1:]],
        out_specs=out_specs,
        out_shape=outs,
        scratch_shapes=[
            pltpu.VMEM((BLOCK + 8, inner + both), F32),
            pltpu.VMEM((state_n, inner), F32),
            pltpu.VMEM((BLOCK, inner), BF16),
            pltpu.VMEM((padded, LANES), F32),
            pltpu.VMEM((1, LANES), F32),
        ],
        compiler_params=params(),
        name="first_merge" if merging else "first",
    )(*ins)
    stream = made[0] if merging else rows
    xv, bc, pack, prefix, ext = made[-5:]

    spread_out = lax.all_to_all(
        ext.reshape(seq, slab, inner + LANES), "seq", 0, 0, tiled=True
    )

    flops = 2 * length * (features * inner + inner * (BLOCK * 4 + state_n) + BLOCK * state_n)
    def second(start, count, made):
        def at(width):
            return pl.BlockSpec((BLOCK, width), lambda i: (i + start, 0))

        def at_block(spec):
            return pl.BlockSpec(spec.block_shape, lambda i: (i + start, 0, 0))

        kept = [pl.BlockSpec(memory_space=pl.ANY)] * len(made)
        return pl.pallas_call(
            functools.partial(second_kernel, heads, len(made)),
            grid=(count,),
            in_specs=kept
            + [
                at(features),
                whole(gain.shape),
                whole(gate_weight.shape),
                at(inner),
                at(both),
                at_block(pack_spec),
                at_block(prefix_spec),
            ],
            out_specs=[at(inner), at(inner)],
            out_shape=[shape((length, inner), BF16), shape((length, inner), BF16)],
            input_output_aliases={k: k for k in range(len(made))},
            compiler_params=params(),
            cost_estimate=pl.CostEstimate(
                flops=flops * count // blocks,
                bytes_accessed=12 * count * BLOCK * inner,
                transcendentals=count * BLOCK * heads * BLOCK,
            ),
            name="second_rest" if made else "second",
        )(*made, stream, gain, gate_weight, xv, bc, pack, prefix)

    early = blocks // 2 if tiling else blocks
    sg, mixed = second(0, early, [])
    if early < blocks:
        spread_out, sg, mixed = lax.optimization_barrier((spread_out, sg, mixed))
        sg, mixed = second(early, blocks - early, [sg, mixed])

    before = pl.pallas_call(
        prefix_kernel,
        out_shape=shape((seq, slab, inner), BF16),
        in_specs=[pl.BlockSpec(memory_space=pltpu.VMEM)],
        out_specs=pl.BlockSpec(memory_space=pltpu.VMEM),
        compiler_params=pltpu.CompilerParams(vmem_limit_bytes=VMEM_LIMIT),
        name="prefix",
    )(spread_out)
    incoming = lax.all_to_all(before, "seq", 0, 0, tiled=True).reshape(state_n, inner)

    norm = norm_gain[None, :]
    finish = shares == 1
    scratch = [pltpu.VMEM((BLOCK, inner), BF16)]
    if not finish:
        outs = [shape((length, features), F32), shape((length, LANES), F32)]
        out_specs = [rows_of(features), rows_of(LANES)]
    elif tiling:
        outs = shape((length // 4, 4 * features), BF16)
        out_specs = pl.BlockSpec((BLOCK // 4, 4 * features), lambda i: (i, 0))
        scratch += [pltpu.VMEM((features // LANES, BLOCK, LANES), F32)]
    else:
        outs, out_specs = shape((length, features), BF16), rows_of(features)
    result = pl.pallas_call(
        functools.partial(third_kernel, heads, finish, tiling, inner * shares),
        grid=(blocks,),
        in_specs=[
            rows_of(features),
            rows_of(inner),
            rows_of(inner),
            pl.BlockSpec((BLOCK, state_n), lambda i: (i, 1)),
            pack_spec,
            whole((state_n, inner)),
            whole(norm.shape),
            whole(out_weight.shape),
        ],
        out_specs=out_specs,
        out_shape=outs,
        scratch_shapes=scratch,
        compiler_params=params(),
        name="third_tiles" if tiling else "third",
    )(stream, sg, mixed, bc, pack, incoming, norm, out_weight)
    if finish:
        return result
    branch, squares = result
    mean = lax.psum(squares[:, :1], "head") / (inner * shares)
    branch = (branch * lax.rsqrt(mean + EPSILON)).astype(BF16)
    if tiling:
        summed = lax.psum(branch, "head").astype(F32)
        return merge_tiles((stream.astype(F32) + summed).astype(BF16))
    summed = lax.psum_scatter(branch, "head", scatter_dimension=1, tiled=True).astype(F32)
    share = features // shares
    mine = lax.dynamic_slice_in_dim(stream, lax.axis_index("head") * share, share, 1)
    return (mine.astype(F32) + summed).astype(BF16)


def merge_tiles(rows):
    count, width_here = rows.shape
    grid = rows.reshape(count // (2 * ROW_PATCHES), 2, ROW_PATCHES // 2, 2, width_here)
    return grid.transpose(0, 2, 1, 3, 4).reshape(count // 4, 4 * width_here)


def shards(tokens, *weights):
    tiles = mamba(tokens, None, *weights[:11], True)
    return mamba(tiles, weights[11], *weights[12:], False)


def solution(mesh):
    return jax.shard_map(
        shards,
        mesh=mesh,
        in_specs=(
            P("seq", None),
            P(),
            P(None, "head"),
            P(None, "head"),
            P(),
            P(None, "head"),
            P(None, "head"),
            P(),
            P("head"),
            P("head"),
            P("head"),
            P("head", None),
            P(),
            P(),
            P(None, "head"),
            P(None, "head"),
            P(),
            P(None, "head"),
            P(None, "head"),
            P(),
            P("head"),
            P("head"),
            P("head"),
            P("head", None),
        ),
        out_specs=P("seq", "head"),
        check_vma=False,
    )
```
